512 devices in a mesh: seq: 32 (over x, y), batch: 16 (over z, core).
Axes of the slice: x: 4, y: 8, z: 8, core: 2. Of those that a mesh axis runs over, the one named last changes fastest.
Arguments:
- query: bfloat16 [32, 4, 64, 576], P('batch', None, 'seq'), may hold values from -48 to 48
- cache: bfloat16 [32, 65536, 576], P('batch', 'seq'), may hold values from -6 to 6
- lengths: int32 [32], P('batch'), may hold values from 4 to 65536
- value_up: bfloat16 [64, 512, 128], P('batch'), may hold values from -0.25 to 0.25
- out_weight: bfloat16 [8192, 7168], P('batch', 'seq'), may hold values from -0.0625 to 0.0625
Outputs:
- mixed: bfloat16 [32, 4, 7168], P('batch', None, 'seq')
The draws below stay inside these ranges and needn't reach their ends.
All inputs are finite; a program needn't handle non-finite values.
Results may differ from the reference program's by a relative error of at most 0.0075.
Values may be sent and summed in bfloat16 or wider, within the bound.
No kernel may reach another device: no remote copies, remote signals or barrier semaphores. Data moves between devices by JAX's collectives and lax.ppermute only.
A program may use at most 128 MiB of HBM per device.

```python
import jax
import jax.numpy as jnp
from jax import lax

D = 7168
H = 64
LAT = 512
ROPE = 64
NOPE = 128
VDIM = 128
CTX_DEV = 2048
NEXT = 4
CTX = 65536
TOTAL_SEQS = 32
N_SEQ = 32


def cache_rows(key):
    first = jax.random.normal(jax.random.fold_in(key, 2), (TOTAL_SEQS, LAT + ROPE), jnp.float32)
    return jnp.clip(first, -6.0, 6.0)


def draw_cache(key, part):
    first = cache_rows(key)
    key = jax.random.fold_in(key, 11)
    filled = jnp.clip(jax.random.normal(jax.random.fold_in(key, 1), (TOTAL_SEQS, CTX, LAT + ROPE), jnp.float32), -6.0, 6.0)
    filled = filled.at[:, 0].set(first)
    return filled.astype(jnp.bfloat16)


def draw_query(key, part):
    key = jax.random.fold_in(key, 12)
    queries = jnp.clip(jax.random.normal(key, (TOTAL_SEQS, NEXT, H, LAT + ROPE), jnp.float32), -6.0, 6.0)
    return queries.astype(jnp.bfloat16)


def draw_lengths(key, part):
    key = jax.random.fold_in(key, 13)
    values = jax.random.randint(jax.random.fold_in(key, 1), (TOTAL_SEQS,), NEXT, CTX + 1)
    picked = jax.random.randint(jax.random.fold_in(key, 2), (), 0, TOTAL_SEQS)
    return jnp.where(jnp.arange(TOTAL_SEQS) == picked, CTX, values).astype(jnp.int32)


def shard_levels(own_key, extent, shards, smallest, largest):
    def one(dim, shards_of):
        draws = jax.random.uniform(jax.random.fold_in(jax.random.fold_in(own_key, 6), dim), (shards_of,), jnp.float32, smallest / len(shards), largest / len(shards))
        return jnp.repeat(jnp.exp(draws), extent[dim] // shards_of).reshape((-1,) + (1,) * (len(extent) - dim - 1))

    factor_of = one(*shards[0])
    for cut in shards[1:]:
        factor_of = factor_of * one(*cut)
    return factor_of


def bell_draw(own_key, extent, spread, reach, pieces=(), kind=jnp.bfloat16):
    array = jax.random.normal(own_key, extent, jnp.float32) * spread
    if len(pieces) > 0:
        array = shard_levels(own_key, extent, pieces, -0.22, 0.18) * array
    return jnp.clip(array, min=-reach, max=reach).astype(kind)


def setup_inputs(seed: int = 0) -> dict:
    seeds = jax.random.split(jax.random.key(seed), 6)
    return {
        "query": draw_query(jax.random.fold_in(seeds[5], 71), 0),
        "cache": draw_cache(jax.random.fold_in(seeds[5], 71), 0),
        "lengths": draw_lengths(jax.random.fold_in(seeds[5], 71), 0),
        "value_up": bell_draw(seeds[3], (H, LAT, VDIM), LAT ** -0.5, 0.25, ((0, 16),)),
        "out_weight": bell_draw(seeds[4], (H * VDIM, D), (H * VDIM) ** -0.5, 0.0625, ((0, 16), (1, 32))),
    }


NEG = -1e30


def attend(item):
    queries, rows, length = item
    scale = 1.0 / (NOPE + ROPE) ** 0.5
    blocks = rows.reshape(N_SEQ, CTX_DEV, LAT + ROPE).astype(jnp.float32)
    scores = jnp.einsum('thk,npk->thnp', queries.astype(jnp.float32), blocks) * scale
    position = jnp.arange(CTX, dtype=jnp.int32).reshape(N_SEQ, CTX_DEV)
    limit = length - NEXT + 1 + jnp.arange(NEXT, dtype=jnp.int32)
    allowed = position[None, None, :, :] < limit[:, None, None, None]
    masked = jnp.where(allowed, scores, NEG)
    block_top = jnp.max(masked, axis=3)
    weights = jnp.where(allowed, jnp.exp(masked - block_top[..., None]), 0.0)
    block_total = jnp.sum(weights, axis=3)
    rounded = weights.astype(jnp.bfloat16).astype(jnp.float32)
    block_out = jnp.einsum('thnp,npl->thnl', rounded, blocks[:, :, :LAT])
    top = jnp.max(block_top, axis=2)
    factor = jnp.exp(block_top - top[..., None])
    total = jnp.sum(block_total * factor, axis=2)
    summed = jnp.sum(block_out * factor[..., None], axis=2)
    return (summed / total[..., None]).astype(jnp.bfloat16)


def reference(query, cache, lengths, value_up, out_weight):
    attended = lax.map(attend, (query, cache, lengths))
    values = jnp.einsum('bthl,hlv->bthv', attended.astype(jnp.float32), value_up.astype(jnp.float32)).astype(jnp.bfloat16)
    flat = values.reshape(TOTAL_SEQS * NEXT, H * VDIM)
    mixed = jnp.dot(flat, out_weight, preferred_element_type=jnp.float32)
    return mixed.reshape(TOTAL_SEQS, NEXT, D).astype(jnp.bfloat16)
```

```python
import jax
import jax.numpy as jnp
from jax import lax
from jax.sharding import PartitionSpec as P

ROPE = 64
NOPE = 128


NEG = -1e30


def per_device(query, cache, lengths, value_up, out_weight):
    n_seq = lax.axis_size("seq")
    n_batch = lax.axis_size("batch")
    seqs, ahead, own, width = query.shape
    ctx_dev = cache.shape[1]
    held, latent, vdim = value_up.shape
    scale = 1.0 / (NOPE + ROPE) ** 0.5
    seq = lax.axis_index("seq")

    rows = lax.all_gather(out_weight, "batch", axis=0, tiled=True)
    per_group = held // own
    part = lax.rem(seq, per_group) * own
    mine = lax.dynamic_slice_in_dim(value_up, part, own, 0)
    pairs = []
    for s in range(n_seq):
        for g in range(n_batch):
            source = (per_group * g + s % per_group) * n_batch + s // per_group
            pairs.append((source, s * n_batch + g))
    up = lax.ppermute(mine, ("seq", "batch"), pairs)

    sent = query.reshape(1, seqs, ahead * own, width)
    queries = lax.all_to_all(
        jnp.broadcast_to(sent, (n_seq,) + sent.shape[1:]), "seq", 0, 0, tiled=True
    )
    scores = (
        jnp.einsum("sbrk,bpk->bsrp", queries, cache, preferred_element_type=jnp.float32) * scale
    )
    position = seq * ctx_dev + jnp.arange(ctx_dev, dtype=jnp.int32)
    limit = lengths[:, None] - ahead + 1 + jnp.arange(ahead * own, dtype=jnp.int32)[None, :] // own
    allowed = position[None, None, None, :] < limit[:, None, :, None]
    masked = jnp.where(allowed, scores, NEG)
    block_top = jnp.max(masked, axis=3).astype(jnp.bfloat16)
    weights = jnp.where(allowed, jnp.exp(masked - block_top.astype(jnp.float32)[..., None]), 0.0)
    block_total = jnp.sum(weights, axis=3)
    block_out = jnp.einsum(
        "bsrp,bpl->bsrl",
        weights.astype(jnp.bfloat16),
        cache[:, :, :latent],
        preferred_element_type=jnp.float32,
    )
    high = block_total.astype(jnp.bfloat16)
    low = (block_total - high.astype(jnp.float32)).astype(jnp.bfloat16)
    extra = jnp.stack([block_top, high, low], axis=-1)
    extra = jnp.pad(extra, ((0, 0), (0, 0), (0, 0), (0, 125)))
    parts = jnp.concatenate([block_out.astype(jnp.bfloat16), extra], axis=-1)
    parts = lax.all_to_all(parts.transpose(1, 0, 2, 3), "seq", 0, 0, tiled=True).astype(jnp.float32)
    block_top, block_total = parts[..., latent], parts[..., latent + 1] + parts[..., latent + 2]
    factor = jnp.exp(block_top - jnp.max(block_top, axis=0))
    total = jnp.sum(block_total * factor, axis=0)
    attended = jnp.sum(parts[..., :latent] * factor[..., None], axis=0) / total[..., None]
    attended = attended.astype(jnp.bfloat16).reshape(seqs, ahead, own, latent)
    values = jnp.einsum(
        "bthl,hlv->bthv", attended, up, preferred_element_type=jnp.float32
    ).astype(jnp.bfloat16)
    values = lax.all_to_all(
        jnp.broadcast_to(values[None], (n_seq,) + values.shape), "seq", 0, 0, tiled=True
    )
    flat = values.transpose(1, 2, 0, 3, 4).reshape(seqs, ahead, n_seq * own * vdim)
    return jnp.einsum("btk,kd->btd", flat, rows, preferred_element_type=jnp.float32).astype(
        jnp.bfloat16
    )


def solution(mesh):
    placed = (
        P("batch", None, "seq", None),
        P("batch", "seq", None),
        P("batch"),
        P("batch", None, None),
        P("batch", "seq"),
    )
    return jax.shard_map(
        per_device, mesh=mesh, in_specs=placed, out_specs=P("batch", None, "seq"), check_vma=False
    )
```

```python
import functools

import jax
import jax.numpy as jnp
from jax import lax
from jax.experimental import pallas as pl
from jax.experimental.pallas import tpu as pltpu
from jax.sharding import Mesh
from jax.sharding import PartitionSpec as P

ROPE = 64
NOPE = 128


NEG = -1e30
LANES = 128
CHUNKS = 8
VMEM = pl.BlockSpec(memory_space=pltpu.VMEM)
SMEM = pl.BlockSpec(memory_space=pltpu.SMEM)


def split(value, pieces):
    out = []
    for _ in range(pieces):
        piece = value.astype(jnp.bfloat16).astype(jnp.float32)
        out.append(piece)
        value = value - piece
    return out


def spread_kernel(scalars_ref, q_ref, out_ref):
    del scalars_ref
    seqs, ahead, own, width = q_ref.shape
    whole = width // LANES
    rest = []
    for b in range(seqs):
        rows = [q_ref[b, t, h : h + 1].astype(jnp.float32) for h in range(own) for t in range(ahead)]
        rows = jnp.concatenate(rows, axis=0)
        for c in range(whole):
            block = rows[:, c * LANES : (c + 1) * LANES].astype(out_ref.dtype)
            out_ref[:, b * whole + c] = jnp.broadcast_to(block[None], out_ref.shape[:1] + block.shape)
        rest.append(rows[:, whole * LANES :])
    rest = jnp.concatenate(rest, axis=1).astype(out_ref.dtype)
    out_ref[:, seqs * whole] = jnp.broadcast_to(rest[None], out_ref.shape[:1] + rest.shape)


def attend_kernel(own, ahead, scalars_ref, q_ref, keys_ref, out_ref):
    n_seq, _, rows, _ = q_ref.shape
    seqs, width, ctx_dev = keys_ref.shape
    whole, left = width // LANES, width % LANES
    latent = (out_ref.shape[2] - 1) * LANES
    all_rows = n_seq * rows
    scale = 1.0 / (NOPE + ROPE) ** 0.5
    base2 = scale * 1.4426950408889634
    row = lax.broadcasted_iota(jnp.int32, (all_rows, 1), 0)
    step = lax.rem(row, ahead)
    position = lax.broadcasted_iota(jnp.int32, (all_rows, ctx_dev), 1)
    lane = lax.broadcasted_iota(jnp.int32, (all_rows, LANES), 1)
    shift = scalars_ref[seqs + 1]
    scores = []
    for b in range(seqs):
        blocks = [q_ref[:, b * whole + c].reshape(all_rows, LANES) for c in range(whole)]
        rest = q_ref[:, seqs * whole].reshape(all_rows, LANES)
        queries = jnp.concatenate(blocks + [rest[:, b * left : (b + 1) * left]], axis=1)
        scores.append(jnp.dot(queries, keys_ref[b], preferred_element_type=jnp.float32))
    for b in range(seqs):
        limit = scalars_ref[b] - ahead + 1 - scalars_ref[seqs] + step
        masked = jnp.where(position < limit, scores[b], NEG)
        top = jnp.max(masked, axis=1, keepdims=True)
        weights = jnp.exp2((masked - jnp.maximum(top, 0.1 * NEG)) * base2)
        total = jnp.sum(weights, axis=1, keepdims=True)
        out = lax.dot_general(
            weights.astype(jnp.bfloat16),
            keys_ref[b, :latent],
            (((1,), (1,)), ((), ())),
            preferred_element_type=jnp.float32,
        )
        extra = jnp.zeros((all_rows, LANES), jnp.float32)
        for at, piece in enumerate(split(top * scale, 3) + split(total, 2)):
            extra = jnp.where(lane == at, piece, extra)
        out = out.astype(jnp.bfloat16)
        extra = extra.astype(jnp.bfloat16)
        for p in range(n_seq):
            owner = lax.rem(p + shift, n_seq)
            pair = slice(p * rows, (p + 1) * rows)
            for c in range(latent // LANES):
                out_ref[owner, b, c] = out[pair, c * LANES : (c + 1) * LANES]
            out_ref[owner, b, latent // LANES] = extra[pair]


def combine_kernel(own, ahead, parts_ref, up_ref, out_ref):
    n_seq, seqs, blocks, rows, _ = parts_ref.shape
    attended = []
    for b in range(seqs):
        extra = parts_ref[:, b, blocks - 1].astype(jnp.float32)
        top = extra[:, :, 0:1] + extra[:, :, 1:2] + extra[:, :, 2:3]
        total = extra[:, :, 3:4] + extra[:, :, 4:5]
        factor = jnp.exp(top - jnp.max(top, axis=0, keepdims=True))
        total = jnp.sum(total * factor, axis=0)
        latents = []
        for c in range(blocks - 1):
            latents.append(jnp.sum(parts_ref[:, b, c].astype(jnp.float32) * factor, axis=0) / total)
        attended.append(jnp.concatenate(latents, axis=1))
    values = []
    for h in range(own):
        mine = [one[h * ahead : (h + 1) * ahead] for one in attended]
        mine = jnp.concatenate(mine + mine, axis=0).astype(jnp.bfloat16)
        one = jnp.dot(mine, up_ref[h], preferred_element_type=jnp.float32)
        values.append(one[: seqs * ahead])
    values = jnp.concatenate(values, axis=0).astype(jnp.bfloat16)
    out_ref[...] = jnp.broadcast_to(values[None], out_ref.shape)


def project_kernel(own, shift_ref, values_ref, weight_ref, out_ref):
    n_seq, rows, vdim = values_ref.shape
    seqs, ahead, _ = out_ref.shape
    columns = weight_ref.shape[0]
    depth = weight_ref.shape[1] // CHUNKS
    steps = rows // own
    pairs = depth // (own * vdim)
    row = lax.broadcasted_iota(jnp.int32, (rows, 1), 0)
    kept = [row // steps == h for h in range(own)]
    out = jnp.zeros((rows, columns), jnp.float32)
    for k in range(CHUNKS):
        flat = []
        for p in range(pairs):
            owner = lax.rem(k * pairs + p + shift_ref[0], n_seq)
            value = values_ref[owner].astype(jnp.float32)
            flat += [jnp.where(one, value, 0.0).astype(jnp.bfloat16) for one in kept]
        out += lax.dot_general(
            jnp.concatenate(flat, axis=1),
            weight_ref[:, k * depth : (k + 1) * depth],
            (((1,), (1,)), ((), ())),
            preferred_element_type=jnp.float32,
        )
    out = sum(out[h * steps : (h + 1) * steps] for h in range(own)).astype(out_ref.dtype)
    for b in range(seqs):
        out_ref[b] = out[b * ahead : (b + 1) * ahead]


def call(kernel, shape, dtype, specs, *operands, scratch=(), limit=24):
    return pl.pallas_call(
        kernel,
        out_shape=jax.ShapeDtypeStruct(shape, dtype),
        in_specs=specs,
        out_specs=VMEM,
        scratch_shapes=scratch,
        compiler_params=pltpu.CompilerParams(vmem_limit_bytes=limit * 1024 * 1024),
    )(*operands)


def per_device(query, cache, lengths, value_up, out_weight):
    n_seq = lax.axis_size("seq")
    chips, cores = lax.axis_size("z"), lax.axis_size("core")
    n_batch = chips * cores
    seqs, ahead, own, width = query.shape
    ctx_dev = cache.shape[1]
    held, latent, vdim = value_up.shape
    seq = lax.axis_index("seq")
    group = lax.axis_index("z") * cores + lax.axis_index("core")
    rows = ahead * own
    bf16 = jnp.bfloat16
    per_group = held // own
    shift = (per_group * group).astype(jnp.int32).reshape(1)

    scalars = jnp.concatenate([lengths, (seq * ctx_dev).astype(jnp.int32).reshape(1), shift])
    queries = call(spread_kernel, (n_seq, seqs * width // LANES, rows, LANES), bf16, [SMEM, VMEM], scalars, query)
    queries = lax.all_to_all(queries, "seq", 0, 0, tiled=True)

    weight = lax.all_gather(out_weight, ("z", "core"), axis=0, tiled=True).T
    mine = lax.dynamic_slice_in_dim(value_up, lax.rem(seq, per_group) * own, own, 0)
    pairs = []
    for s in range(n_seq):
        for g in range(n_batch):
            pairs.append((s * n_batch + (s // per_group - g) % n_batch, s * n_batch + g))
    up = lax.ppermute(mine, ("seq", "z", "core"), pairs)

    parts = call(
        functools.partial(attend_kernel, own, ahead),
        (n_seq, seqs, latent // LANES + 1, rows, LANES),
        bf16,
        [SMEM, VMEM, VMEM],
        scalars,
        queries,
        cache.swapaxes(1, 2),
    )
    parts = lax.all_to_all(parts, "seq", 0, 0, tiled=True)
    values = call(
        functools.partial(combine_kernel, own, ahead),
        (n_seq, seqs * rows, vdim),
        bf16,
        [VMEM, VMEM],
        parts,
        up,
    )
    values = lax.all_to_all(values, "seq", 0, 0, tiled=True)
    return call(
        functools.partial(project_kernel, own),
        (seqs, ahead, out_weight.shape[1]),
        bf16,
        [SMEM, VMEM, VMEM],
        shift,
        values,
        weight,
    )


def solution(mesh):
    n_seq, n_batch = mesh.devices.shape
    split_mesh = Mesh(mesh.devices.reshape(n_seq, n_batch // 2, 2), ("seq", "z", "core"))
    batch = ("z", "core")
    placed = (
        P(batch, None, "seq", None),
        P(batch, "seq", None),
        P(batch),
        P(batch, None, None),
        P(batch, "seq"),
    )
    return jax.shard_map(
        per_device, mesh=split_mesh, in_specs=placed, out_specs=P(batch, None, "seq"), check_vma=False
    )
```

```python
import functools

import jax
import jax.numpy as jnp
from jax import lax
from jax.experimental import pallas as pl
from jax.experimental.pallas import tpu as pltpu
from jax.sharding import Mesh
from jax.sharding import PartitionSpec as P

ROPE = 64
NOPE = 128


NEG = -1e30
LANES = 128
PARTS = 4
PIECES = 5
VMEM = pl.BlockSpec(memory_space=pltpu.VMEM)
HBM = pl.BlockSpec(memory_space=pltpu.HBM)
SMEM = pl.BlockSpec(memory_space=pltpu.SMEM)


def owner_of(pair, n_seq, chips, start, core):
    at_chip = n_seq // chips
    half = at_chip // 2
    chip, rest = lax.div(pair, at_chip), lax.rem(pair, at_chip)
    swapped = lax.rem(lax.div(rest, half) + core, 2)
    return lax.rem(chip + start, chips) * at_chip + swapped * half + lax.rem(rest, half)


def split(value, pieces):
    out = []
    for _ in range(pieces):
        piece = value.astype(jnp.bfloat16).astype(jnp.float32)
        out.append(piece)
        value = value - piece
    return out


def spread_kernel(q_ref, out_ref):
    seqs, ahead, own, width = q_ref.shape
    whole = width // LANES
    rest = []
    for b in range(seqs):
        rows = [q_ref[b, t, h : h + 1].astype(jnp.float32) for h in range(own) for t in range(ahead)]
        rows = jnp.concatenate(rows, axis=0)
        for c in range(whole):
            block = rows[:, c * LANES : (c + 1) * LANES].astype(out_ref.dtype)
            out_ref[:, b * whole + c] = jnp.broadcast_to(block[None], out_ref.shape[:1] + block.shape)
        rest.append(rows[:, whole * LANES :])
    rest = jnp.concatenate(rest, axis=1).astype(out_ref.dtype)
    out_ref[:, seqs * whole] = jnp.broadcast_to(rest[None], out_ref.shape[:1] + rest.shape)


def attend_kernel(own, ahead, chips, scalars_ref, q_ref, cache_ref, up_ref, out_ref, keys_ref, sems):
    del up_ref
    n_seq, _, rows, _ = q_ref.shape
    seqs, width, ctx_dev = keys_ref.shape
    whole, left = width // LANES, width % LANES
    latent = (out_ref.shape[1] - 1) // seqs * LANES
    all_rows = n_seq * rows
    scale = 1.0 / (NOPE + ROPE) ** 0.5
    base2 = scale * 1.4426950408889634
    row = lax.broadcasted_iota(jnp.int32, (all_rows, 1), 0)
    step = lax.rem(row, ahead)
    position = lax.broadcasted_iota(jnp.int32, (all_rows, ctx_dev), 1)
    lane = lax.broadcasted_iota(jnp.int32, (all_rows, LANES), 1)
    start, core = scalars_ref[seqs + 1], scalars_ref[seqs + 2]
    part = ctx_dev // PARTS
    copies = {}
    for b in range(seqs):
        for k in range(PARTS):
            at = pl.ds(k * part, part)
            copies[b, k] = pltpu.make_async_copy(
                cache_ref.at[b, :, at], keys_ref.at[b, :, at], sems.at[b, k]
            )
    for k in range(PARTS):
        copies[0, k].start()
    extra = jnp.zeros((all_rows, LANES), jnp.float32)
    for b in range(seqs):
        blocks = [q_ref[:, b * whole + c].reshape(all_rows, LANES) for c in range(whole)]
        rest = q_ref[:, seqs * whole].reshape(all_rows, LANES)
        queries = jnp.concatenate(blocks + [rest[:, b * left : (b + 1) * left]], axis=1)
        scores = []
        for k in range(PARTS):
            copies[b, k].wait()
            if b + 1 < seqs:
                copies[b + 1, k].start()
            keys = keys_ref[b, :, k * part : (k + 1) * part]
            scores.append(jnp.dot(queries, keys, preferred_element_type=jnp.float32))
        scores = jnp.concatenate(scores, axis=1)
        limit = scalars_ref[b] - ahead + 1 - scalars_ref[seqs] + step
        masked = jnp.where(position < limit, scores, NEG)
        top = jnp.max(masked, axis=1, keepdims=True)
        weights = jnp.exp2((masked - jnp.maximum(top, 0.1 * NEG)) * base2)
        total = jnp.sum(weights, axis=1, keepdims=True)
        out = lax.dot_general(
            weights.astype(jnp.bfloat16),
            keys_ref[b, :latent],
            (((1,), (1,)), ((), ())),
            preferred_element_type=jnp.float32,
        )
        for at, piece in enumerate(split(top * scale, 3) + split(total, 2)):
            extra = jnp.where(lane == PIECES * b + at, piece, extra)
        out = out.astype(jnp.bfloat16)
        for p in range(n_seq):
            owner = owner_of(p, n_seq, chips, start, core)
            for c in range(latent // LANES):
                block = out[p * rows : (p + 1) * rows, c * LANES : (c + 1) * LANES]
                out_ref[owner, b * (latent // LANES) + c] = block
    extra = extra.astype(jnp.bfloat16)
    for p in range(n_seq):
        owner = owner_of(p, n_seq, chips, start, core)
        out_ref[owner, seqs * (latent // LANES)] = extra[p * rows : (p + 1) * rows]


def combine_kernel(own, ahead, parts_ref, up_ref, out_ref):
    n_seq, blocks, rows, _ = parts_ref.shape
    seqs = out_ref.shape[1] // rows
    each = (blocks - 1) // seqs
    extra = parts_ref[:, blocks - 1].astype(jnp.float32)
    attended = []
    for b in range(seqs):
        piece = [extra[:, :, PIECES * b + k : PIECES * b + k + 1] for k in range(PIECES)]
        top = piece[0] + piece[1] + piece[2]
        total = piece[3] + piece[4]
        factor = jnp.exp(top - jnp.max(top, axis=0, keepdims=True))
        total = jnp.sum(total * factor, axis=0)
        latents = []
        for c in range(each):
            latents.append(jnp.sum(parts_ref[:, each * b + c].astype(jnp.float32) * factor, axis=0) / total)
        attended.append(jnp.concatenate(latents, axis=1))
    values = []
    for h in range(own):
        mine = [one[h * ahead : (h + 1) * ahead] for one in attended]
        mine = jnp.concatenate(mine + mine, axis=0).astype(jnp.bfloat16)
        one = jnp.dot(mine, up_ref[h], preferred_element_type=jnp.float32)
        values.append(one[: seqs * ahead])
    values = jnp.concatenate(values, axis=0).astype(jnp.bfloat16)
    out_ref[...] = jnp.broadcast_to(values[None], out_ref.shape)


def project_kernel(own, chips, cores, place_ref, values_ref, *refs):
    *weight_refs, out_ref = refs
    _, n_seq, rows, vdim = values_ref.shape
    steps = rows // own
    pairs = n_seq // (chips * cores)
    row = lax.broadcasted_iota(jnp.int32, (cores * rows, 1), 0)
    kept = [lax.rem(row, rows) // steps == h for h in range(own)]
    chip, core = place_ref[0], place_ref[1]

    def term(weight, at, c):
        flat = []
        for p in range(pairs):
            pair = (at * cores + c) * pairs + p
            value = []
            for g in range(cores):
                start = lax.rem((chips - 3) * chip + chips // 2 * g, chips)
                value.append(values_ref[g, owner_of(pair, n_seq, chips, start, g)].astype(jnp.float32))
            value = jnp.concatenate(value, axis=0)
            flat += [jnp.where(one, value, 0.0).astype(jnp.bfloat16) for one in kept]
        return lax.dot_general(
            jnp.concatenate(flat, axis=1),
            weight,
            (((1,), (1,)), ((), ())),
            preferred_element_type=jnp.float32,
        )

    last = len(weight_refs) - 1
    out = term(weight_refs[0][...], chip, core)
    for k in range(1, last):
        at = lax.rem(jnp.where(core == 0, chip + chips - k, chip + k), chips)
        for c in range(cores):
            out += term(weight_refs[k][c], at, c)
    out += term(weight_refs[last][...], lax.rem(chip + last, chips), core)
    for g in range(cores):
        out_ref[g] = sum(out[g * rows + h * steps : g * rows + (h + 1) * steps] for h in range(own))


def exchange(blocks):
    flat = blocks.reshape(blocks.shape[0], -1, LANES)
    return lax.all_to_all(flat, "seq", 0, 0, tiled=True).reshape(blocks.shape)


def call(kernel, shape, dtype, specs, *operands, scratch=(), limit=24):
    return pl.pallas_call(
        kernel,
        out_shape=jax.ShapeDtypeStruct(shape, dtype),
        in_specs=specs,
        out_specs=VMEM,
        scratch_shapes=scratch,
        compiler_params=pltpu.CompilerParams(vmem_limit_bytes=limit * 1024 * 1024),
    )(*operands)


def per_device(query, cache, lengths, value_up, out_weight):
    n_seq = lax.axis_size("seq")
    chips, cores = lax.axis_size("z"), lax.axis_size("core")
    n_batch = chips * cores
    seqs, ahead, own, width = query.shape
    ctx_dev = cache.shape[1]
    held, latent, vdim = value_up.shape
    seq = lax.axis_index("seq")
    rows = ahead * own
    bf16 = jnp.bfloat16
    per_group = held // own
    z, core = lax.axis_index("z"), lax.axis_index("core")
    place = jnp.stack([lax.rem((chips - 3) * z + chips // 2 * core, chips), core]).astype(jnp.int32)
    scalars = jnp.concatenate([lengths, (seq * ctx_dev).astype(jnp.int32).reshape(1), place])

    blocks = seqs * (latent // LANES) + 1
    queries = call(spread_kernel, (n_seq, blocks, rows, LANES), bf16, [VMEM], query)
    queries = exchange(queries)

    ring = [
        (chip * cores + c, (chip + 1 - 2 * c) % chips * cores + c)
        for chip in range(chips)
        for c in range(cores)
    ]
    batch = ("z", "core")
    block = lax.all_gather(out_weight.T, "core")
    weights = [out_weight.T]
    for _ in range(chips // 2 - 1):
        block = lax.ppermute(block, batch, ring)
        weights.append(block)
    weights.append(lax.ppermute(lax.dynamic_index_in_dim(block, core, 0, False), batch, ring))
    mine = lax.dynamic_slice_in_dim(value_up, lax.rem(seq, per_group) * own, own, 0)
    pairs = []
    for s in range(n_seq):
        at, swap = s // (n_seq // chips), s // per_group % cores
        for to in range(chips):
            for c in range(cores):
                source = (3 * to + chips // 2 * c + at) % chips * cores + (c + swap) % cores
                pairs.append((s * n_batch + source, (s * chips + to) * cores + c))
    up = lax.ppermute(mine, ("seq", "z", "core"), pairs)

    parts = call(
        functools.partial(attend_kernel, own, ahead, chips),
        (n_seq, blocks, rows, LANES),
        bf16,
        [SMEM, VMEM, HBM, VMEM],
        scalars,
        queries,
        cache.swapaxes(1, 2),
        up[:, :16],
        scratch=[
            pltpu.VMEM((seqs, width, ctx_dev), bf16),
            pltpu.SemaphoreType.DMA((seqs, PARTS)),
        ],
        limit=52,
    )
    parts = exchange(parts)
    values = call(
        functools.partial(combine_kernel, own, ahead),
        (n_seq, seqs * rows, vdim),
        bf16,
        [VMEM, VMEM],
        parts,
        up,
    )
    values = exchange(values)
    terms = call(
        functools.partial(project_kernel, own, chips, cores),
        (cores, seqs * ahead, out_weight.shape[1]),
        jnp.float32,
        [SMEM, VMEM] + [VMEM] * len(weights),
        jnp.stack([z, core]).astype(jnp.int32),
        lax.all_gather(values, "core"),
        *weights,
    )
    terms = lax.all_gather(terms, "core")
    out = lax.dynamic_index_in_dim(terms, core, 1, False).sum(axis=0)
    return out.reshape(seqs, ahead, out_weight.shape[1]).astype(bf16)


def solution(mesh):
    n_seq, n_batch = mesh.devices.shape
    split_mesh = Mesh(mesh.devices.reshape(n_seq, n_batch // 2, 2), ("seq", "z", "core"))
    batch = ("z", "core")
    placed = (
        P(batch, None, "seq", None),
        P(batch, "seq", None),
        P(batch),
        P(batch, None, None),
        P(batch, "seq"),
    )
    return jax.shard_map(
        per_device, mesh=split_mesh, in_specs=placed, out_specs=P(batch, None, "seq"), check_vma=False
    )
```

```python
import functools

import jax
import jax.numpy as jnp
from jax import lax
from jax.experimental import pallas as pl
from jax.experimental.pallas import tpu as pltpu
from jax.sharding import Mesh
from jax.sharding import PartitionSpec as P

ROPE = 64
NOPE = 128


NEG = -1e30
LANES = 128
PIECES = 5
VMEM = pl.BlockSpec(memory_space=pltpu.VMEM)
HBM = pl.BlockSpec(memory_space=pltpu.HBM)
SMEM = pl.BlockSpec(memory_space=pltpu.SMEM)


def owner_of(pair, n_seq, chips, start, core):
    at_chip = n_seq // chips
    half = at_chip // 2
    chip, rest = lax.div(pair, at_chip), lax.rem(pair, at_chip)
    swapped = lax.rem(lax.div(rest, half) + core, 2)
    return lax.rem(chip + start, chips) * at_chip + swapped * half + lax.rem(rest, half)


def split(value, pieces):
    out = []
    for _ in range(pieces):
        piece = value.astype(jnp.bfloat16).astype(jnp.float32)
        out.append(piece)
        value = value - piece
    return out


def spread_kernel(q_ref, out_ref):
    seqs, ahead, own, width = q_ref.shape
    whole = width // LANES
    rest = []
    for b in range(seqs):
        rows = [q_ref[b, t, h : h + 1].astype(jnp.float32) for h in range(own) for t in range(ahead)]
        rows = jnp.concatenate(rows, axis=0)
        for c in range(whole):
            block = rows[:, c * LANES : (c + 1) * LANES].astype(out_ref.dtype)
            out_ref[:, b * whole + c] = jnp.broadcast_to(block[None], out_ref.shape[:1] + block.shape)
        rest.append(rows[:, whole * LANES :])
    rest = jnp.concatenate(rest, axis=1).astype(out_ref.dtype)
    out_ref[:, seqs * whole] = jnp.broadcast_to(rest[None], out_ref.shape[:1] + rest.shape)


def attend_kernel(own, ahead, chips, scalars_ref, q_ref, cache_ref, up_ref, out_ref, keys_ref, sems):
    del up_ref
    n_seq, _, rows, _ = q_ref.shape
    seqs, width, ctx_dev = keys_ref.shape
    whole, left = width // LANES, width % LANES
    latent = (out_ref.shape[1] - 1) // seqs * LANES
    all_rows = n_seq * rows
    scale = 1.0 / (NOPE + ROPE) ** 0.5
    base2 = scale * 1.4426950408889634
    row = lax.broadcasted_iota(jnp.int32, (all_rows, 1), 0)
    step = lax.rem(row, ahead)
    position = lax.broadcasted_iota(jnp.int32, (all_rows, ctx_dev), 1)
    lane = lax.broadcasted_iota(jnp.int32, (all_rows, LANES), 1)
    start, core = scalars_ref[seqs + 1], scalars_ref[seqs + 2]
    copies = [pltpu.make_async_copy(cache_ref.at[b], keys_ref.at[b], sems.at[b]) for b in range(seqs)]
    copies[0].start()
    extra = jnp.zeros((all_rows, LANES), jnp.float32)
    for b in range(seqs):
        blocks = [q_ref[:, b * whole + c].reshape(all_rows, LANES) for c in range(whole)]
        rest = q_ref[:, seqs * whole].reshape(all_rows, LANES)
        queries = jnp.concatenate(blocks + [rest[:, b * left : (b + 1) * left]], axis=1)
        copies[b].wait()
        if b + 1 < seqs:
            copies[b + 1].start()
        scores = jnp.dot(queries, keys_ref[b], preferred_element_type=jnp.float32)
        limit = scalars_ref[b] - ahead + 1 - scalars_ref[seqs] + step
        masked = jnp.where(position < limit, scores, NEG)
        top = jnp.max(masked, axis=1, keepdims=True)
        weights = jnp.exp2((masked - jnp.maximum(top, 0.1 * NEG)) * base2)
        total = jnp.sum(weights, axis=1, keepdims=True)
        out = lax.dot_general(
            weights.astype(jnp.bfloat16),
            keys_ref[b, :latent],
            (((1,), (1,)), ((), ())),
            preferred_element_type=jnp.float32,
        )
        for at, piece in enumerate(split(top * scale, 3) + split(total, 2)):
            extra = jnp.where(lane == PIECES * b + at, piece, extra)
        out = out.astype(jnp.bfloat16)
        for p in range(n_seq):
            owner = owner_of(p, n_seq, chips, start, core)
            for c in range(latent // LANES):
                block = out[p * rows : (p + 1) * rows, c * LANES : (c + 1) * LANES]
                out_ref[owner, b * (latent // LANES) + c] = block
    extra = extra.astype(jnp.bfloat16)
    for p in range(n_seq):
        owner = owner_of(p, n_seq, chips, start, core)
        out_ref[owner, seqs * (latent // LANES)] = extra[p * rows : (p + 1) * rows]


def combine_kernel(own, ahead, parts_ref, up_ref, out_ref):
    n_seq, blocks, rows, _ = parts_ref.shape
    seqs = out_ref.shape[1] // rows
    each = (blocks - 1) // seqs
    extra = parts_ref[:, blocks - 1].astype(jnp.float32)
    attended = []
    for b in range(seqs):
        piece = [extra[:, :, PIECES * b + k : PIECES * b + k + 1] for k in range(PIECES)]
        top = piece[0] + piece[1] + piece[2]
        total = piece[3] + piece[4]
        factor = jnp.exp(top - jnp.max(top, axis=0, keepdims=True))
        total = jnp.sum(total * factor, axis=0)
        latents = []
        for c in range(each):
            latents.append(jnp.sum(parts_ref[:, each * b + c].astype(jnp.float32) * factor, axis=0) / total)
        attended.append(jnp.concatenate(latents, axis=1))
    values = []
    for h in range(own):
        mine = [one[h * ahead : (h + 1) * ahead] for one in attended]
        mine = jnp.concatenate(mine + mine, axis=0).astype(jnp.bfloat16)
        one = jnp.dot(mine, up_ref[h], preferred_element_type=jnp.float32)
        values.append(one[: seqs * ahead])
    values = jnp.concatenate(values, axis=0).astype(jnp.bfloat16)
    out_ref[...] = jnp.broadcast_to(values[None], out_ref.shape)


def project_kernel(own, chips, cores, place_ref, values_ref, *refs):
    *weight_refs, out_ref = refs
    _, n_seq, rows, vdim = values_ref.shape
    steps = rows // own
    pairs = n_seq // (chips * cores)
    row = lax.broadcasted_iota(jnp.int32, (cores * rows, 1), 0)
    kept = [lax.rem(row, rows) // steps == h for h in range(own)]
    chip, core = place_ref[0], place_ref[1]

    def term(weight, at, c):
        flat = []
        for p in range(pairs):
            pair = (at * cores + c) * pairs + p
            value = []
            for g in range(cores):
                start = lax.rem((chips - 3) * chip + chips // 2 * g, chips)
                value.append(values_ref[g, owner_of(pair, n_seq, chips, start, g)].astype(jnp.float32))
            value = jnp.concatenate(value, axis=0)
            flat += [jnp.where(one, value, 0.0).astype(jnp.bfloat16) for one in kept]
        return lax.dot_general(
            jnp.concatenate(flat, axis=1),
            weight,
            (((1,), (1,)), ((), ())),
            preferred_element_type=jnp.float32,
        )

    last = len(weight_refs) - 1
    out = term(weight_refs[0][...], chip, core)
    for k in range(1, last):
        at = lax.rem(jnp.where(core == 0, chip + chips - k, chip + k), chips)
        for c in range(cores):
            out += term(weight_refs[k][c], at, c)
    out += term(weight_refs[last][...], lax.rem(chip + last, chips), core)
    for g in range(cores):
        out_ref[g] = sum(out[g * rows + h * steps : g * rows + (h + 1) * steps] for h in range(own))


def exchange(blocks):
    flat = blocks.reshape(blocks.shape[0], -1, LANES)
    return lax.all_to_all(flat, "seq", 0, 0, tiled=True).reshape(blocks.shape)


def call(kernel, shape, dtype, specs, *operands, scratch=(), limit=24):
    return pl.pallas_call(
        kernel,
        out_shape=jax.ShapeDtypeStruct(shape, dtype),
        in_specs=specs,
        out_specs=VMEM,
        scratch_shapes=scratch,
        compiler_params=pltpu.CompilerParams(vmem_limit_bytes=limit * 1024 * 1024),
    )(*operands)


def per_device(query, cache, lengths, value_up, out_weight):
    n_seq = lax.axis_size("seq")
    chips, cores = lax.axis_size("z"), lax.axis_size("core")
    n_batch = chips * cores
    seqs, ahead, own, width = query.shape
    ctx_dev = cache.shape[1]
    held, latent, vdim = value_up.shape
    seq = lax.axis_index("seq")
    rows = ahead * own
    bf16 = jnp.bfloat16
    per_group = held // own
    z, core = lax.axis_index("z"), lax.axis_index("core")
    place = jnp.stack([lax.rem((chips - 3) * z + chips // 2 * core, chips), core]).astype(jnp.int32)
    scalars = jnp.concatenate([lengths, (seq * ctx_dev).astype(jnp.int32).reshape(1), place])

    blocks = seqs * (latent // LANES) + 1
    queries = call(spread_kernel, (n_seq, blocks, rows, LANES), bf16, [VMEM], query)
    queries = exchange(queries)

    ring = [
        (chip * cores + c, (chip + 1 - 2 * c) % chips * cores + c)
        for chip in range(chips)
        for c in range(cores)
    ]
    batch = ("z", "core")
    block = lax.all_gather(out_weight.T, "core")
    weights = [out_weight.T]
    for _ in range(chips // 2 - 1):
        block = lax.ppermute(block, batch, ring)
        weights.append(block)
    weights.append(lax.ppermute(lax.dynamic_index_in_dim(block, core, 0, False), batch, ring))
    mine = lax.dynamic_slice_in_dim(value_up, lax.rem(seq, per_group) * own, own, 0)
    pairs = []
    for s in range(n_seq):
        at, swap = s // (n_seq // chips), s // per_group % cores
        for to in range(chips):
            for c in range(cores):
                source = (3 * to + chips // 2 * c + at) % chips * cores + (c + swap) % cores
                pairs.append((s * n_batch + source, (s * chips + to) * cores + c))
    up = lax.ppermute(mine, ("seq", "z", "core"), pairs)

    parts = call(
        functools.partial(attend_kernel, own, ahead, chips),
        (n_seq, blocks, rows, LANES),
        bf16,
        [SMEM, VMEM, HBM, VMEM],
        scalars,
        queries,
        cache.swapaxes(1, 2),
        up[:, :16],
        scratch=[
            pltpu.VMEM((seqs, width, ctx_dev), bf16),
            pltpu.SemaphoreType.DMA((seqs,)),
        ],
        limit=52,
    )
    parts = exchange(parts)
    values = call(
        functools.partial(combine_kernel, own, ahead),
        (n_seq, seqs * rows, vdim),
        bf16,
        [VMEM, VMEM],
        parts,
        up,
    )
    values = exchange(values)
    terms = call(
        functools.partial(project_kernel, own, chips, cores),
        (cores, seqs * ahead, out_weight.shape[1]),
        jnp.float32,
        [SMEM, VMEM] + [VMEM] * len(weights),
        jnp.stack([z, core]).astype(jnp.int32),
        lax.all_gather(values, "core"),
        *weights,
    )
    terms = lax.all_gather(terms, "core")
    out = lax.dynamic_index_in_dim(terms, core, 1, False).sum(axis=0)
    return out.reshape(seqs, ahead, out_weight.shape[1]).astype(bf16)


def solution(mesh):
    n_seq, n_batch = mesh.devices.shape
    split_mesh = Mesh(mesh.devices.reshape(n_seq, n_batch // 2, 2), ("seq", "z", "core"))
    batch = ("z", "core")
    placed = (
        P(batch, None, "seq", None),
        P(batch, "seq", None),
        P(batch),
        P(batch, None, None),
        P(batch, "seq"),
    )
    return jax.shard_map(
        per_device, mesh=split_mesh, in_specs=placed, out_specs=P(batch, None, "seq"), check_vma=False
    )
```

```python
import functools

import jax
import jax.numpy as jnp
from jax import lax
from jax.experimental import pallas as pl
from jax.experimental.pallas import tpu as pltpu
from jax.sharding import Mesh
from jax.sharding import PartitionSpec as P

ROPE = 64
NOPE = 128


NEG = -1e30
LANES = 128
PIECES = 5
PARTS = 4
VMEM = pl.BlockSpec(memory_space=pltpu.VMEM)
HBM = pl.BlockSpec(memory_space=pltpu.HBM)
SMEM = pl.BlockSpec(memory_space=pltpu.SMEM)


def owner_of(pair, n_seq, chips, start, core):
    at_chip = n_seq // chips
    half = at_chip // 2
    chip, rest = lax.div(pair, at_chip), lax.rem(pair, at_chip)
    swapped = lax.rem(lax.div(rest, half) + core, 2)
    return lax.rem(chip + start, chips) * at_chip + swapped * half + lax.rem(rest, half)


def split(value, pieces):
    out = []
    for _ in range(pieces):
        piece = value.astype(jnp.bfloat16).astype(jnp.float32)
        out.append(piece)
        value = value - piece
    return out


def spread_kernel(q_ref, out_ref):
    seqs, ahead, own, width = q_ref.shape
    whole = width // LANES
    rest = []
    for b in range(seqs):
        rows = [q_ref[b, t, h : h + 1].astype(jnp.float32) for h in range(own) for t in range(ahead)]
        rows = jnp.concatenate(rows, axis=0)
        for c in range(whole):
            block = rows[:, c * LANES : (c + 1) * LANES].astype(out_ref.dtype)
            out_ref[:, b * whole + c] = jnp.broadcast_to(block[None], out_ref.shape[:1] + block.shape)
        rest.append(rows[:, whole * LANES :])
    rest = jnp.concatenate(rest, axis=1).astype(out_ref.dtype)
    out_ref[:, seqs * whole] = jnp.broadcast_to(rest[None], out_ref.shape[:1] + rest.shape)


def attend_kernel(own, ahead, chips, scalars_ref, q_ref, cache_ref, up_ref, out_ref, keys_ref, sems):
    del up_ref
    n_seq, _, rows, _ = q_ref.shape
    seqs, width, ctx_dev = keys_ref.shape
    whole, left = width // LANES, width % LANES
    latent = (out_ref.shape[1] - 1) // seqs * LANES
    all_rows = n_seq * rows
    scale = 1.0 / (NOPE + ROPE) ** 0.5
    base2 = scale * 1.4426950408889634
    row = lax.broadcasted_iota(jnp.int32, (all_rows, 1), 0)
    step = lax.rem(row, ahead)
    lane = lax.broadcasted_iota(jnp.int32, (all_rows, LANES), 1)
    start, core = scalars_ref[seqs + 1], scalars_ref[seqs + 2]
    copies = [pltpu.make_async_copy(cache_ref.at[b], keys_ref.at[b], sems.at[b]) for b in range(seqs)]
    for copy in copies:
        copy.start()
    part = ctx_dev // PARTS
    rest = q_ref[:, seqs * whole].reshape(all_rows, LANES)

    def masked_scores(b, k):
        blocks = [q_ref[:, b * whole + c].reshape(all_rows, LANES) for c in range(whole)]
        queries = jnp.concatenate(blocks + [rest[:, b * left : (b + 1) * left]], axis=1)
        keys = keys_ref[b, :, k * part : (k + 1) * part]
        scores = jnp.dot(queries, keys, preferred_element_type=jnp.float32)
        limit = scalars_ref[b] - ahead + 1 - scalars_ref[seqs] + step
        position = lax.broadcasted_iota(jnp.int32, (all_rows, part), 1) + k * part
        return jnp.where(position < limit, scores, NEG)

    extra = jnp.zeros((all_rows, LANES), jnp.float32)
    copies[0].wait()
    scores = [masked_scores(0, k) for k in range(PARTS)]
    for b in range(seqs):
        if b + 1 < seqs:
            copies[b + 1].wait()
        top = jnp.max(scores[0], axis=1, keepdims=True)
        for one in scores[1:]:
            top = jnp.maximum(top, jnp.max(one, axis=1, keepdims=True))
        total = jnp.zeros((all_rows, 1), jnp.float32)
        out = jnp.zeros((all_rows, latent), jnp.float32)
        following = []
        for k in range(PARTS):
            weights = jnp.exp2((scores[k] - jnp.maximum(top, 0.1 * NEG)) * base2)
            total += jnp.sum(weights, axis=1, keepdims=True)
            out += lax.dot_general(
                weights.astype(jnp.bfloat16),
                keys_ref[b, :latent, k * part : (k + 1) * part],
                (((1,), (1,)), ((), ())),
                preferred_element_type=jnp.float32,
            )
            if b + 1 < seqs:
                following.append(masked_scores(b + 1, k))
        scores = following
        for at, piece in enumerate(split(top * scale, 3) + split(total, 2)):
            extra = jnp.where(lane == PIECES * b + at, piece, extra)
        out = out.astype(jnp.bfloat16)
        for p in range(n_seq):
            owner = owner_of(p, n_seq, chips, start, core)
            for c in range(latent // LANES):
                block = out[p * rows : (p + 1) * rows, c * LANES : (c + 1) * LANES]
                out_ref[owner, b * (latent // LANES) + c] = block
    extra = extra.astype(jnp.bfloat16)
    for p in range(n_seq):
        owner = owner_of(p, n_seq, chips, start, core)
        out_ref[owner, seqs * (latent // LANES)] = extra[p * rows : (p + 1) * rows]


def combine_kernel(own, ahead, parts_ref, up_ref, out_ref):
    n_seq, blocks, rows, _ = parts_ref.shape
    seqs = out_ref.shape[1] // rows
    each = (blocks - 1) // seqs
    extra = parts_ref[:, blocks - 1].astype(jnp.float32)
    attended = []
    for b in range(seqs):
        piece = [extra[:, :, PIECES * b + k : PIECES * b + k + 1] for k in range(PIECES)]
        top = piece[0] + piece[1] + piece[2]
        total = piece[3] + piece[4]
        factor = jnp.exp(top - jnp.max(top, axis=0, keepdims=True))
        total = jnp.sum(total * factor, axis=0)
        latents = []
        for c in range(each):
            latents.append(jnp.sum(parts_ref[:, each * b + c].astype(jnp.float32) * factor, axis=0) / total)
        attended.append(jnp.concatenate(latents, axis=1))
    values = []
    for h in range(own):
        mine = [one[h * ahead : (h + 1) * ahead] for one in attended]
        mine = jnp.concatenate(mine + mine, axis=0).astype(jnp.bfloat16)
        one = jnp.dot(mine, up_ref[h], preferred_element_type=jnp.float32)
        values.append(one[: seqs * ahead])
    values = jnp.concatenate(values, axis=0).astype(jnp.bfloat16)
    out_ref[...] = jnp.broadcast_to(values[None], out_ref.shape)


def project_kernel(own, chips, cores, place_ref, values_ref, *refs):
    *weight_refs, out_ref = refs
    _, n_seq, rows, vdim = values_ref.shape
    steps = rows // own
    pairs = n_seq // (chips * cores)
    row = lax.broadcasted_iota(jnp.int32, (cores * rows, 1), 0)
    kept = [lax.rem(row, rows) // steps == h for h in range(own)]
    chip, core = place_ref[0], place_ref[1]

    def term(weight, at, c):
        flat = []
        for p in range(pairs):
            pair = (at * cores + c) * pairs + p
            value = []
            for g in range(cores):
                start = lax.rem((chips - 3) * chip + chips // 2 * g, chips)
                value.append(values_ref[g, owner_of(pair, n_seq, chips, start, g)].astype(jnp.float32))
            value = jnp.concatenate(value, axis=0)
            flat += [jnp.where(one, value, 0.0).astype(jnp.bfloat16) for one in kept]
        return lax.dot_general(
            jnp.concatenate(flat, axis=1),
            weight,
            (((1,), (1,)), ((), ())),
            preferred_element_type=jnp.float32,
        )

    last = len(weight_refs) - 1
    out = term(weight_refs[0][...], chip, core)
    for k in range(1, last):
        at = lax.rem(jnp.where(core == 0, chip + chips - k, chip + k), chips)
        for c in range(cores):
            out += term(weight_refs[k][c], at, c)
    out += term(weight_refs[last][...], lax.rem(chip + last, chips), core)
    for g in range(cores):
        out_ref[g] = sum(out[g * rows + h * steps : g * rows + (h + 1) * steps] for h in range(own))


def exchange(blocks):
    flat = blocks.reshape(blocks.shape[0], -1, LANES)
    return lax.all_to_all(flat, "seq", 0, 0, tiled=True).reshape(blocks.shape)


def call(kernel, shape, dtype, specs, *operands, scratch=(), limit=24):
    return pl.pallas_call(
        kernel,
        out_shape=jax.ShapeDtypeStruct(shape, dtype),
        in_specs=specs,
        out_specs=VMEM,
        scratch_shapes=scratch,
        compiler_params=pltpu.CompilerParams(vmem_limit_bytes=limit * 1024 * 1024),
    )(*operands)


def per_device(query, cache, lengths, value_up, out_weight):
    n_seq = lax.axis_size("seq")
    chips, cores = lax.axis_size("z"), lax.axis_size("core")
    n_batch = chips * cores
    seqs, ahead, own, width = query.shape
    ctx_dev = cache.shape[1]
    held, latent, vdim = value_up.shape
    seq = lax.axis_index("seq")
    rows = ahead * own
    bf16 = jnp.bfloat16
    per_group = held // own
    z, core = lax.axis_index("z"), lax.axis_index("core")
    place = jnp.stack([lax.rem((chips - 3) * z + chips // 2 * core, chips), core]).astype(jnp.int32)
    scalars = jnp.concatenate([lengths, (seq * ctx_dev).astype(jnp.int32).reshape(1), place])

    blocks = seqs * (latent // LANES) + 1
    queries = call(spread_kernel, (n_seq, blocks, rows, LANES), bf16, [VMEM], query)
    queries = exchange(queries)

    ring = [
        (chip * cores + c, (chip + 1 - 2 * c) % chips * cores + c)
        for chip in range(chips)
        for c in range(cores)
    ]
    batch = ("z", "core")
    block = lax.all_gather(out_weight.T, "core")
    weights = [out_weight.T]
    for _ in range(chips // 2 - 1):
        block = lax.ppermute(block, batch, ring)
        weights.append(block)
    weights.append(lax.ppermute(lax.dynamic_index_in_dim(block, core, 0, False), batch, ring))
    mine = lax.dynamic_slice_in_dim(value_up, lax.rem(seq, per_group) * own, own, 0)
    pairs = []
    for s in range(n_seq):
        at, swap = s // (n_seq // chips), s // per_group % cores
        for to in range(chips):
            for c in range(cores):
                source = (3 * to + chips // 2 * c + at) % chips * cores + (c + swap) % cores
                pairs.append((s * n_batch + source, (s * chips + to) * cores + c))
    up = lax.ppermute(mine, ("seq", "z", "core"), pairs)

    parts = call(
        functools.partial(attend_kernel, own, ahead, chips),
        (n_seq, blocks, rows, LANES),
        bf16,
        [SMEM, VMEM, HBM, VMEM],
        scalars,
        queries,
        cache.swapaxes(1, 2),
        up[:, :16],
        scratch=[
            pltpu.VMEM((seqs, width, ctx_dev), bf16),
            pltpu.SemaphoreType.DMA((seqs,)),
        ],
        limit=52,
    )
    parts = exchange(parts)
    values = call(
        functools.partial(combine_kernel, own, ahead),
        (n_seq, seqs * rows, vdim),
        bf16,
        [VMEM, VMEM],
        parts,
        up,
    )
    values = exchange(values)
    terms = call(
        functools.partial(project_kernel, own, chips, cores),
        (cores, seqs * ahead, out_weight.shape[1]),
        jnp.float32,
        [SMEM, VMEM] + [VMEM] * len(weights),
        jnp.stack([z, core]).astype(jnp.int32),
        lax.all_gather(values, "core"),
        *weights,
    )
    terms = lax.all_gather(terms, "core")
    out = lax.dynamic_index_in_dim(terms, core, 1, False).sum(axis=0)
    return out.reshape(seqs, ahead, out_weight.shape[1]).astype(bf16)


def solution(mesh):
    n_seq, n_batch = mesh.devices.shape
    split_mesh = Mesh(mesh.devices.reshape(n_seq, n_batch // 2, 2), ("seq", "z", "core"))
    batch = ("z", "core")
    placed = (
        P(batch, None, "seq", None),
        P(batch, "seq", None),
        P(batch),
        P(batch, None, None),
        P(batch, "seq"),
    )
    return jax.shard_map(
        per_device, mesh=split_mesh, in_specs=placed, out_specs=P(batch, None, "seq"), check_vma=False
    )
```

```python
import functools

import jax
import jax.numpy as jnp
from jax import lax
from jax.experimental import pallas as pl
from jax.experimental.pallas import tpu as pltpu
from jax.sharding import Mesh
from jax.sharding import PartitionSpec as P

ROPE = 64
NOPE = 128


NEG = -1e30
LANES = 128
PIECES = 5
PARTS = 4
VMEM = pl.BlockSpec(memory_space=pltpu.VMEM)
HBM = pl.BlockSpec(memory_space=pltpu.HBM)
SMEM = pl.BlockSpec(memory_space=pltpu.SMEM)


def owner_of(pair, n_seq, chips, start, core):
    at_chip = n_seq // chips
    half = at_chip // 2
    chip, rest = lax.div(pair, at_chip), lax.rem(pair, at_chip)
    swapped = lax.rem(lax.div(rest, half) + core, 2)
    return lax.rem(chip + start, chips) * at_chip + swapped * half + lax.rem(rest, half)


def split(value, pieces):
    out = []
    for _ in range(pieces):
        piece = value.astype(jnp.bfloat16).astype(jnp.float32)
        out.append(piece)
        value = value - piece
    return out


def spread_kernel(q_ref, out_ref):
    seqs, ahead, own, width = q_ref.shape
    whole = width // LANES
    rest = []
    for b in range(seqs):
        rows = [q_ref[b, t, h : h + 1].astype(jnp.float32) for h in range(own) for t in range(ahead)]
        rows = jnp.concatenate(rows, axis=0)
        for c in range(whole):
            block = rows[:, c * LANES : (c + 1) * LANES].astype(out_ref.dtype)
            out_ref[:, b * whole + c] = jnp.broadcast_to(block[None], out_ref.shape[:1] + block.shape)
        rest.append(rows[:, whole * LANES :])
    rest = jnp.concatenate(rest, axis=1).astype(out_ref.dtype)
    out_ref[:, seqs * whole] = jnp.broadcast_to(rest[None], out_ref.shape[:1] + rest.shape)


def attend_kernel(own, ahead, chips, scalars_ref, q_ref, cache_ref, up_ref, out_ref, keys_ref, sems):
    del up_ref
    n_seq, _, rows, _ = q_ref.shape
    seqs, width, ctx_dev = keys_ref.shape
    whole, left = width // LANES, width % LANES
    latent = (out_ref.shape[1] - 1) // seqs * LANES
    all_rows = n_seq * rows
    scale = 1.0 / (NOPE + ROPE) ** 0.5
    base2 = scale * 1.4426950408889634
    row = lax.broadcasted_iota(jnp.int32, (all_rows, 1), 0)
    step = lax.rem(row, ahead)
    lane = lax.broadcasted_iota(jnp.int32, (all_rows, LANES), 1)
    start, core = scalars_ref[seqs + 1], scalars_ref[seqs + 2]
    copies = []
    for b in range(seqs):
        pieces = PARTS if b == 0 else 1
        size = width // pieces
        for k in range(pieces):
            at = pl.ds(k * size, size)
            copies.append(
                pltpu.make_async_copy(cache_ref.at[b, at], keys_ref.at[b, at], sems.at[len(copies)])
            )
            copies[-1].start()
    part = ctx_dev // PARTS
    rest = q_ref[:, seqs * whole].reshape(all_rows, LANES)

    def masked_scores(b, k):
        blocks = [q_ref[:, b * whole + c].reshape(all_rows, LANES) for c in range(whole)]
        queries = jnp.concatenate(blocks + [rest[:, b * left : (b + 1) * left]], axis=1)
        keys = keys_ref[b, :, k * part : (k + 1) * part]
        scores = jnp.dot(queries, keys, preferred_element_type=jnp.float32)
        limit = scalars_ref[b] - ahead + 1 - scalars_ref[seqs] + step
        position = lax.broadcasted_iota(jnp.int32, (all_rows, part), 1) + k * part
        return jnp.where(position < limit, scores, NEG)

    extra = jnp.zeros((all_rows, LANES), jnp.float32)
    for copy in copies[:PARTS]:
        copy.wait()
    scores = [masked_scores(0, k) for k in range(PARTS)]
    for b in range(seqs):
        if b + 1 < seqs:
            copies[PARTS + b].wait()
        top = jnp.max(scores[0], axis=1, keepdims=True)
        for one in scores[1:]:
            top = jnp.maximum(top, jnp.max(one, axis=1, keepdims=True))
        total = jnp.zeros((all_rows, 1), jnp.float32)
        out = jnp.zeros((all_rows, latent), jnp.float32)
        following = []
        for k in range(PARTS):
            weights = jnp.exp2((scores[k] - jnp.maximum(top, 0.1 * NEG)) * base2)
            total += jnp.sum(weights, axis=1, keepdims=True)
            out += lax.dot_general(
                weights.astype(jnp.bfloat16),
                keys_ref[b, :latent, k * part : (k + 1) * part],
                (((1,), (1,)), ((), ())),
                preferred_element_type=jnp.float32,
            )
            if b + 1 < seqs:
                following.append(masked_scores(b + 1, k))
        scores = following
        for at, piece in enumerate(split(top * scale, 3) + split(total, 2)):
            extra = jnp.where(lane == PIECES * b + at, piece, extra)
        out = out.astype(jnp.bfloat16)
        for p in range(n_seq):
            owner = owner_of(p, n_seq, chips, start, core)
            for c in range(latent // LANES):
                block = out[p * rows : (p + 1) * rows, c * LANES : (c + 1) * LANES]
                out_ref[owner, b * (latent // LANES) + c] = block
    extra = extra.astype(jnp.bfloat16)
    for p in range(n_seq):
        owner = owner_of(p, n_seq, chips, start, core)
        out_ref[owner, seqs * (latent // LANES)] = extra[p * rows : (p + 1) * rows]


def combine_kernel(own, ahead, parts_ref, up_ref, out_ref):
    n_seq, blocks, rows, _ = parts_ref.shape
    seqs = out_ref.shape[1] // rows
    each = (blocks - 1) // seqs
    extra = parts_ref[:, blocks - 1].astype(jnp.float32)
    attended = []
    for b in range(seqs):
        piece = [extra[:, :, PIECES * b + k : PIECES * b + k + 1] for k in range(PIECES)]
        top = piece[0] + piece[1] + piece[2]
        total = piece[3] + piece[4]
        factor = jnp.exp(top - jnp.max(top, axis=0, keepdims=True))
        total = jnp.sum(total * factor, axis=0)
        latents = []
        for c in range(each):
            latents.append(jnp.sum(parts_ref[:, each * b + c].astype(jnp.float32) * factor, axis=0) / total)
        attended.append(jnp.concatenate(latents, axis=1))
    values = []
    for h in range(own):
        mine = [one[h * ahead : (h + 1) * ahead] for one in attended]
        mine = jnp.concatenate(mine + mine, axis=0).astype(jnp.bfloat16)
        one = jnp.dot(mine, up_ref[h], preferred_element_type=jnp.float32)
        values.append(one[: seqs * ahead])
    values = jnp.concatenate(values, axis=0).astype(jnp.bfloat16)
    out_ref[...] = jnp.broadcast_to(values[None], out_ref.shape)


def project_kernel(own, chips, cores, place_ref, values_ref, *refs):
    *weight_refs, out_ref = refs
    _, n_seq, rows, vdim = values_ref.shape
    steps = rows // own
    pairs = n_seq // (chips * cores)
    row = lax.broadcasted_iota(jnp.int32, (cores * rows, 1), 0)
    kept = [lax.rem(row, rows) // steps == h for h in range(own)]
    chip, core = place_ref[0], place_ref[1]

    def term(weight, at, c):
        flat = []
        for p in range(pairs):
            pair = (at * cores + c) * pairs + p
            value = []
            for g in range(cores):
                start = lax.rem((chips - 3) * chip + chips // 2 * g, chips)
                value.append(values_ref[g, owner_of(pair, n_seq, chips, start, g)].astype(jnp.float32))
            value = jnp.concatenate(value, axis=0)
            flat += [jnp.where(one, value, 0.0).astype(jnp.bfloat16) for one in kept]
        return lax.dot_general(
            jnp.concatenate(flat, axis=1),
            weight,
            (((1,), (1,)), ((), ())),
            preferred_element_type=jnp.float32,
        )

    last = len(weight_refs) - 1
    out = term(weight_refs[0][...], chip, core)
    for k in range(1, last):
        at = lax.rem(jnp.where(core == 0, chip + chips - k, chip + k), chips)
        for c in range(cores):
            out += term(weight_refs[k][c], at, c)
    out += term(weight_refs[last][...], lax.rem(chip + last, chips), core)
    for g in range(cores):
        out_ref[g] = sum(out[g * rows + h * steps : g * rows + (h + 1) * steps] for h in range(own))


def exchange(blocks):
    flat = blocks.reshape(blocks.shape[0], -1, LANES)
    return lax.all_to_all(flat, "seq", 0, 0, tiled=True).reshape(blocks.shape)


def call(kernel, shape, dtype, specs, *operands, scratch=(), limit=24):
    return pl.pallas_call(
        kernel,
        out_shape=jax.ShapeDtypeStruct(shape, dtype),
        in_specs=specs,
        out_specs=VMEM,
        scratch_shapes=scratch,
        compiler_params=pltpu.CompilerParams(vmem_limit_bytes=limit * 1024 * 1024),
    )(*operands)


def per_device(query, cache, lengths, value_up, out_weight):
    n_seq = lax.axis_size("seq")
    chips, cores = lax.axis_size("z"), lax.axis_size("core")
    n_batch = chips * cores
    seqs, ahead, own, width = query.shape
    ctx_dev = cache.shape[1]
    held, latent, vdim = value_up.shape
    seq = lax.axis_index("seq")
    rows = ahead * own
    bf16 = jnp.bfloat16
    per_group = held // own
    z, core = lax.axis_index("z"), lax.axis_index("core")
    place = jnp.stack([lax.rem((chips - 3) * z + chips // 2 * core, chips), core]).astype(jnp.int32)
    scalars = jnp.concatenate([lengths, (seq * ctx_dev).astype(jnp.int32).reshape(1), place])

    blocks = seqs * (latent // LANES) + 1
    queries = call(spread_kernel, (n_seq, blocks, rows, LANES), bf16, [VMEM], query)
    queries = exchange(queries)

    ring = [
        (chip * cores + c, (chip + 1 - 2 * c) % chips * cores + c)
        for chip in range(chips)
        for c in range(cores)
    ]
    batch = ("z", "core")
    block = lax.all_gather(out_weight.T, "core")
    weights = [out_weight.T]
    for _ in range(chips // 2 - 1):
        block = lax.ppermute(block, batch, ring)
        weights.append(block)
    weights.append(lax.ppermute(lax.dynamic_index_in_dim(block, core, 0, False), batch, ring))
    mine = lax.dynamic_slice_in_dim(value_up, lax.rem(seq, per_group) * own, own, 0)
    pairs = []
    for s in range(n_seq):
        at, swap = s // (n_seq // chips), s // per_group % cores
        for to in range(chips):
            for c in range(cores):
                source = (3 * to + chips // 2 * c + at) % chips * cores + (c + swap) % cores
                pairs.append((s * n_batch + source, (s * chips + to) * cores + c))
    up = lax.ppermute(mine, ("seq", "z", "core"), pairs)

    parts = call(
        functools.partial(attend_kernel, own, ahead, chips),
        (n_seq, blocks, rows, LANES),
        bf16,
        [SMEM, VMEM, HBM, VMEM],
        scalars,
        queries,
        cache.swapaxes(1, 2),
        up[:, :16],
        scratch=[
            pltpu.VMEM((seqs, width, ctx_dev), bf16),
            pltpu.SemaphoreType.DMA((PARTS + seqs - 1,)),
        ],
        limit=52,
    )
    parts = exchange(parts)
    values = call(
        functools.partial(combine_kernel, own, ahead),
        (n_seq, seqs * rows, vdim),
        bf16,
        [VMEM, VMEM],
        parts,
        up,
    )
    values = exchange(values)
    terms = call(
        functools.partial(project_kernel, own, chips, cores),
        (cores, seqs * ahead, out_weight.shape[1]),
        jnp.float32,
        [SMEM, VMEM] + [VMEM] * len(weights),
        jnp.stack([z, core]).astype(jnp.int32),
        lax.all_gather(values, "core"),
        *weights,
    )
    terms = lax.all_gather(terms, "core")
    out = lax.dynamic_index_in_dim(terms, core, 1, False).sum(axis=0)
    return out.reshape(seqs, ahead, out_weight.shape[1]).astype(bf16)


def solution(mesh):
    n_seq, n_batch = mesh.devices.shape
    split_mesh = Mesh(mesh.devices.reshape(n_seq, n_batch // 2, 2), ("seq", "z", "core"))
    batch = ("z", "core")
    placed = (
        P(batch, None, "seq", None),
        P(batch, "seq", None),
        P(batch),
        P(batch, None, None),
        P(batch, "seq"),
    )
    return jax.shard_map(
        per_device, mesh=split_mesh, in_specs=placed, out_specs=P(batch, None, "seq"), check_vma=False
    )
```
